32 devices in a mesh: rep: 4 (over y, core), fsdp: 8 (over z, x).
Axes of the slice: x: 2, y: 2, z: 4, core: 2. Of those that a mesh axis runs over, the one named last changes fastest.
Arguments:
- grads: bfloat16 [4, 2, 512, 8192], P('rep', None, 'fsdp'), may hold values from -0.29882812 to 0.29882812
- left_stat: float32 [32, 512, 512], P(('rep', 'fsdp')), may hold values from -6 to 6
- right_stat: float32 [32, 512, 512], P(('rep', 'fsdp')), may hold values from -6 to 6
- left_root: bfloat16 [32, 512, 512], P(('rep', 'fsdp')), may hold values from -1 to 3
- right_root: bfloat16 [32, 512, 512], P(('rep', 'fsdp')), may hold values from -1 to 3
- accum: float32 [32, 512, 512], P(('rep', 'fsdp')), may hold values from 0.01 to 1
Outputs:
- update: bfloat16 [2, 512, 8192], P(None, 'fsdp', 'rep')
- left_new: float32 [32, 512, 512], P(('rep', 'fsdp'))
- right_new: float32 [32, 512, 512], P(('rep', 'fsdp'))
- accum_new: float32 [32, 512, 512], P(('rep', 'fsdp'))
The draws below stay inside these ranges and needn't reach their ends.
All inputs are finite; a program needn't handle non-finite values.
Results may differ from the reference program's by a relative error of at most 0.02.
Values may be sent and summed in bfloat16 or wider, within the bound.
No kernel may reach another device: no remote copies, remote signals or barrier semaphores. Data moves between devices by JAX's collectives and lax.ppermute only.
A program may use at most 64 MiB of HBM per device.

```python
import math
import jax
import jax.numpy as jnp
from jax import lax

WIDTH = 8192
BS = 512
NB = 32
SLABS = 2
N_REP = 4


def root_matrix(key, low, high):
    first, second = jax.random.split(key)
    base = jax.random.truncated_normal(first, -4.0, 4.0, (NB, BS, BS), jnp.float32) * (0.7 / BS ** 0.5)
    mirror = 0.5 * (base + jnp.swapaxes(base, 1, 2))
    diag_vals = jax.random.uniform(second, (NB, BS, 1), jnp.float32, low, high)
    rows = jnp.arange(BS)[:, None]
    cols = jnp.arange(BS)[None, :]
    ident = (rows == cols).astype(jnp.float32)
    return mirror + diag_vals * ident[None, :, :]


def draw_left_root(key, part):
    key = jax.random.fold_in(key, 11)
    return root_matrix(key, 0.5, 1.5).astype(jnp.bfloat16)


def draw_right_root(key, part):
    key = jax.random.fold_in(key, 23)
    return root_matrix(key, 0.5, 1.5).astype(jnp.bfloat16)


def level_of(own_key, dims, pieces, least, largest):
    factor_of, own = 1.0, jax.random.fold_in(own_key, 6)
    for position, parts in pieces:
        heights = jnp.exp(jax.random.uniform(jax.random.fold_in(own, position), (parts,), jnp.float32, least / len(pieces), largest / len(pieces)))
        factor_of = factor_of * jnp.repeat(heights, dims[position] // parts).reshape([-1 if axis == position else 1 for axis in range(len(dims))])
    return factor_of


def noise(rng, shape, deviation, reach, cuts=(), held_as=jnp.bfloat16):
    array = deviation * jax.random.normal(rng, shape, jnp.float32)
    if cuts:
        array = array * level_of(rng, shape, cuts, -0.22, 0.18)
    return jnp.clip(array, -reach, reach).astype(held_as)


def setup_inputs(seed: int = 0) -> dict:
    streams_of = jax.random.split(jax.random.key(seed), 7)
    grads = noise(streams_of[0], (N_REP, SLABS, BS, WIDTH), 0.05, 0.29882812, ((0, 4), (2, 8)))
    left_stat = noise(streams_of[1], (NB, BS, BS), 1.0, 6.0, ((0, 32),), jnp.float32)
    right_stat = noise(streams_of[2], (NB, BS, BS), 1.0, 6.0, ((0, 32),), jnp.float32)
    left_root = draw_left_root(jax.random.fold_in(streams_of[6], 71), 0)
    right_root = draw_right_root(jax.random.fold_in(streams_of[6], 71), 0)
    accum = jnp.clip(jnp.exp(math.log(1.0) - 4.6051702 * jax.random.uniform(streams_of[5], (NB, BS, BS), jnp.float32) ** level_of(streams_of[5], (NB, BS, BS), ((0, 32),), -0.2, 0.2)), 0.01, 1.0)
    return dict(grads=grads, left_stat=left_stat, right_stat=right_stat, left_root=left_root, right_root=right_root, accum=accum)


def one_block(items):
    grad_block, left, right, lroot, rroot, acc = items
    left_next = left + jnp.dot(grad_block, grad_block.T, precision=lax.Precision.HIGHEST)
    right_next = right + jnp.dot(grad_block.T, grad_block, precision=lax.Precision.HIGHEST)
    acc_next = acc + grad_block * grad_block
    adagrad = grad_block / jnp.sqrt(acc_next)
    blocks_low = grad_block.astype(jnp.bfloat16)
    half = jnp.dot(lroot, blocks_low, preferred_element_type=jnp.float32).astype(jnp.bfloat16)
    precond = jnp.dot(half, rroot, preferred_element_type=jnp.float32)
    ratio = jnp.sqrt(jnp.sum(adagrad * adagrad)) / jnp.sqrt(jnp.sum(precond * precond) + 1e-06)
    return ((ratio * precond).astype(jnp.bfloat16), left_next, right_next, acc_next)

def reference(grads, left_stat, right_stat, left_root, right_root, accum):
    summed = lax.optimization_barrier(jnp.sum(grads.astype(jnp.float32), axis=0))
    slabs, block, width = summed.shape
    bcols = width // block
    blocks = summed.reshape(slabs, block, bcols, block).transpose(2, 0, 1, 3).reshape(bcols * slabs, block, block)
    updates, left_new, right_new, accum_new = lax.map(one_block, (blocks, left_stat, right_stat, left_root, right_root, accum))
    update = updates.reshape(bcols, slabs, block, block).transpose(1, 2, 0, 3).reshape(slabs, block, width)
    return (update, left_new, right_new, accum_new)
```

```python
import functools

import jax
import jax.numpy as jnp
from jax import lax
from jax.experimental import pallas as pl
from jax.experimental.pallas import tpu as pltpu
from jax.sharding import PartitionSpec as P

MIB = 1024 * 1024
ANY = pl.BlockSpec(memory_space=pl.ANY)
VMEM = pl.BlockSpec(memory_space=pltpu.VMEM)


def swap(x, axis, bit):
    n = lax.axis_size(axis)
    return lax.ppermute(x, axis, [(i, i ^ bit) for i in range(n)])


def pick_kernel(fsdp_count, other, grads, half0, half1, sem):
    slabs, width = grads.shape[1], grads.shape[3]
    groups, _, _, cols = half0.shape
    block = 2 * cols
    low = lax.rem(lax.axis_index("rep"), 2)
    low = 1 - low if other else low
    copies = []
    for h, out in enumerate((half0, half1)):
        for g in range(groups):
            for f in range(fsdp_count):
                column = (2 * g + low) * (fsdp_count // slabs) + f // slabs
                start = pl.multiple_of(column * block + h * cols, cols)
                copies.append(
                    pltpu.make_async_copy(
                        grads.at[0, f % slabs, :, pl.ds(start, cols)], out.at[g, f], sem
                    )
                )
    for copy in copies:
        copy.start()
    for copy in copies:
        copy.wait()


def pick(grads, other, rep_count, fsdp_count):
    _, slabs, rows, width = grads.shape
    block = rows * fsdp_count
    shape = jax.ShapeDtypeStruct((rep_count // 2, fsdp_count, rows, block // 2), grads.dtype)
    return pl.pallas_call(
        functools.partial(pick_kernel, fsdp_count, other),
        out_shape=(shape, shape),
        in_specs=[ANY],
        out_specs=(ANY, ANY),
        scratch_shapes=[pltpu.SemaphoreType.DMA],
        compiler_params=pltpu.CompilerParams(vmem_limit_bytes=4 * MIB),
        cost_estimate=pl.CostEstimate(flops=0, bytes_accessed=2 * MIB, transcendentals=0),
        name="pick_other" if other else "pick_own",
    )(grads)


def place(z, x, k, other, rows):
    at = 2 * jnp.bitwise_xor(z, k) + (1 - x if other else x)
    return pl.ds(pl.multiple_of(at * rows, rows), rows)


def main_kernel(peers, *refs):
    firsts = refs[:peers]
    crossed = refs[peers]
    seconds = refs[peers + 1 : 2 * peers + 1]
    left_root, right_root, accum = refs[2 * peers + 1 : 2 * peers + 4]
    outs = refs[2 * peers + 4 :]
    sends, own0, away1, own1, block_out = outs[: peers - 1], *outs[peers - 1 : peers + 3]
    block, lroot, rroot, acc, sems = outs[peers + 3 :]
    rows, cols = firsts[0].shape[1:]
    me = lax.axis_index("fsdp")
    z, x = me // 2, lax.rem(me, 2)

    lcopy = pltpu.make_async_copy(left_root.at[0], lroot, sems.at[1])
    rcopy = pltpu.make_async_copy(right_root.at[0], rroot, sems.at[2])
    acopy = pltpu.make_async_copy(accum.at[0], acc, sems.at[3])
    copies = []
    for k in range(peers):
        here, there = place(z, x, k, False, rows), place(z, x, k, True, rows)
        for src, to, h in (
            (firsts[k].at[x], here, 0),
            (crossed.at[k], there, 0),
            (seconds[k].at[0], here, 1),
            (seconds[k].at[1], there, 1),
        ):
            copies.append(
                pltpu.make_async_copy(src, block.at[to, pl.ds(h * cols, cols)], sems.at[0])
            )
    lcopy.start()
    for copy in copies:
        copy.start()
    rcopy.start()
    acopy.start()
    lcopy.wait()
    for copy in copies:
        copy.wait()
    b = block[...]
    half = jnp.dot(lroot[...], b, preferred_element_type=jnp.float32).astype(jnp.bfloat16)
    rcopy.wait()
    precond = jnp.dot(half, rroot[...], preferred_element_type=jnp.float32)
    acopy.wait()
    wide = b.astype(jnp.float32)
    square = wide * wide
    ada_sq = jnp.sum(square / (acc[...] + square))
    pre_sq = jnp.sum(precond * precond)
    ratio = jnp.sqrt(ada_sq) / jnp.sqrt(pre_sq + 1e-06)
    block_out[...] = b
    lroot[...] = (ratio * precond).astype(jnp.bfloat16)
    lo, hi = pl.ds(0, cols), pl.ds(cols, cols)
    for k in range(peers):
        target = own0 if k == 0 else sends[k - 1]
        for xx in range(2):
            at = 2 * jnp.bitwise_xor(z, k) + xx
            target[xx] = lroot[pl.ds(pl.multiple_of(at * rows, rows), rows), lo]
    for zz in range(peers):
        at = pl.multiple_of((2 * zz + x) * rows, rows)
        own1[zz] = lroot[pl.ds(at, rows), hi]
        at = pl.multiple_of((2 * zz + 1 - x) * rows, rows)
        away1[zz] = lroot[pl.ds(at, rows), hi]


def precondition(firsts, crossed, seconds, left_root, right_root, accum):
    peers = len(firsts)
    side = left_root.shape[1]
    pair = jax.ShapeDtypeStruct(firsts[0].shape, jnp.bfloat16)
    line = jax.ShapeDtypeStruct(crossed.shape, jnp.bfloat16)
    outs = pl.pallas_call(
        functools.partial(main_kernel, peers),
        out_shape=(pair,) * peers + (line, line, jax.ShapeDtypeStruct((side, side), jnp.bfloat16)),
        in_specs=[ANY] * (2 * peers + 4),
        out_specs=(VMEM,) * (peers + 3),
        scratch_shapes=[
            pltpu.VMEM((side, side), jnp.bfloat16),
            pltpu.VMEM((side, side), jnp.bfloat16),
            pltpu.VMEM((side, side), jnp.bfloat16),
            pltpu.VMEM((side, side), jnp.float32),
            pltpu.SemaphoreType.DMA((4,)),
        ],
        compiler_params=pltpu.CompilerParams(vmem_limit_bytes=16 * MIB),
        cost_estimate=pl.CostEstimate(
            flops=4 * side**3, bytes_accessed=12 * side * side, transcendentals=0
        ),
        name="precondition",
    )(*firsts, crossed, *seconds, left_root, right_root, accum)
    return outs[: peers - 1], outs[peers - 1], outs[peers], outs[peers + 1], outs[peers + 2]


def stats_kernel(block, left, right, accum, left_out, right_out, accum_out):
    b = block[...]
    wide = b.astype(jnp.float32)
    accum_out[0] = accum[0] + wide * wide
    left_out[0] = left[0] + lax.dot_general(
        b, b, (((1,), (1,)), ((), ())), preferred_element_type=jnp.float32
    )
    right_out[0] = right[0] + lax.dot_general(
        b, b, (((0,), (0,)), ((), ())), preferred_element_type=jnp.float32
    )


def statistics(block, left, right, accum):
    shape = jax.ShapeDtypeStruct(left.shape, jnp.float32)
    side = left.shape[1]
    return pl.pallas_call(
        stats_kernel,
        out_shape=(shape,) * 3,
        in_specs=[VMEM] * 4,
        out_specs=(VMEM,) * 3,
        compiler_params=pltpu.CompilerParams(vmem_limit_bytes=20 * MIB),
        cost_estimate=pl.CostEstimate(
            flops=4 * side**3, bytes_accessed=26 * side * side, transcendentals=0
        ),
        name="statistics",
    )(block, left, right, accum)


def assemble_kernel(peers, *refs):
    firsts = refs[:peers]
    crossed = refs[peers]
    seconds = refs[peers + 1 : 2 * peers + 1]
    update, sem = refs[2 * peers + 1 :]
    slabs = update.shape[0]
    rows, cols = firsts[0].shape[1:]
    me = lax.axis_index("fsdp")
    z, x = me // 2, lax.rem(me, 2)
    copies = []
    for k in range(peers):
        for h, other, src in (
            (0, False, firsts[k].at[x]),
            (0, True, crossed.at[k]),
            (1, False, seconds[k].at[0]),
            (1, True, seconds[k].at[1]),
        ):
            owner = 2 * jnp.bitwise_xor(z, k) + (1 - x if other else x)
            start = pl.multiple_of((owner // slabs * 2 + h) * cols, cols)
            copies.append(
                pltpu.make_async_copy(
                    src, update.at[lax.rem(owner, slabs), :, pl.ds(start, cols)], sem
                )
            )
    for copy in copies:
        copy.start()
    for copy in copies:
        copy.wait()


def assemble(firsts, crossed, seconds, shape):
    peers = len(firsts)
    return pl.pallas_call(
        functools.partial(assemble_kernel, peers),
        out_shape=jax.ShapeDtypeStruct(shape, jnp.bfloat16),
        in_specs=[ANY] * (2 * peers + 1),
        out_specs=ANY,
        scratch_shapes=[pltpu.SemaphoreType.DMA],
        compiler_params=pltpu.CompilerParams(vmem_limit_bytes=4 * MIB),
        cost_estimate=pl.CostEstimate(flops=0, bytes_accessed=MIB, transcendentals=0),
        name="assemble",
    )(*firsts, crossed, *seconds)


def pick_one(x, index, axis=0):
    return lax.dynamic_index_in_dim(x, index, axis, keepdims=False)


def far_first(peers):
    return sorted(range(1, peers), reverse=True)


def body(grads, left_stat, right_stat, left_root, right_root, accum):
    rep_count, fsdp_count = lax.axis_size("rep"), lax.axis_size("fsdp")
    peers = fsdp_count // 2
    rep, fsdp = lax.axis_index("rep"), lax.axis_index("fsdp")
    z, x = fsdp // 2, fsdp % 2
    slabs, rows, width = grads.shape[1:]
    order = far_first(peers)

    away = pick(grads, True, rep_count, fsdp_count)
    mine = pick(grads, False, rep_count, fsdp_count)

    def add(a, b):
        return (a.astype(jnp.float32) + b.astype(jnp.float32)).astype(jnp.bfloat16)

    summed = []
    for h in range(2):
        part, kept, bit = swap(away[h], "rep", 1), mine[h], 1
        while 2 * bit < rep_count:
            bit *= 2
            side = (rep // bit) % 2
            part, kept = [
                a.reshape((a.shape[0] // 2, 2) + a.shape[1:]) for a in (part, kept)
            ]
            send = add(pick_one(part, 1 - side, 1), pick_one(kept, 1 - side, 1))
            kept = add(pick_one(part, side, 1), pick_one(kept, side, 1))
            part = swap(send, "rep", bit)
        summed.append((part[0], kept[0]))

    def piece(pair):
        return [a.reshape((peers, 2) + a.shape[1:]) for a in pair]

    part, kept = piece(summed[0])
    firsts = [None] * peers
    firsts[0] = add(pick_one(part, z), pick_one(kept, z))
    for k in order:
        send = add(pick_one(part, z ^ k), pick_one(kept, z ^ k))
        firsts[k] = swap(send, "fsdp", 2 * k)
    crossed = swap(jnp.stack([pick_one(a, 1 - x) for a in firsts]), "fsdp", 1)

    part, kept = piece(summed[1])
    stay = add(pick_one(part, x, 1), pick_one(kept, x, 1))
    come = swap(add(pick_one(part, 1 - x, 1), pick_one(kept, 1 - x, 1)), "fsdp", 1)
    seconds = [None] * peers
    for k in [0] + order:
        pair = jnp.stack([pick_one(stay, z ^ k), pick_one(come, z ^ k)])
        seconds[k] = pair if k == 0 else swap(pair, "fsdp", 2 * k)

    sends, own0, away1, own1, block = precondition(
        firsts, crossed, seconds, left_root, right_root, accum
    )

    firsts = [own0] + [None] * (peers - 1)
    for k in order:
        firsts[k] = swap(sends[k - 1], "fsdp", 2 * k)
    come = swap(away1, "fsdp", 1)
    crossed = swap(jnp.stack([pick_one(a, 1 - x) for a in firsts]), "fsdp", 1)
    seconds = [None] * peers
    for k in [0] + order:
        pair = jnp.stack([pick_one(own1, z ^ k), pick_one(come, z ^ k)])
        seconds[k] = pair if k == 0 else swap(pair, "fsdp", 2 * k)

    left_new, right_new, accum_new = statistics(block, left_stat, right_stat, accum)
    update = assemble(firsts, crossed, seconds, (slabs, rows, width // rep_count))
    return (update, left_new, right_new, accum_new)


def solution(mesh):
    owned = P(("rep", "fsdp"), None, None)
    return jax.shard_map(
        body,
        mesh=mesh,
        in_specs=(P("rep", None, "fsdp", None),) + (owned,) * 5,
        out_specs=(P(None, "fsdp", "rep"),) + (owned,) * 3,
        check_vma=False,
    )
```

```python
import functools

import jax
import jax.numpy as jnp
from jax import lax
from jax.experimental import pallas as pl
from jax.experimental.pallas import tpu as pltpu
from jax.sharding import PartitionSpec as P

MIB = 1024 * 1024
ANY = pl.BlockSpec(memory_space=pl.ANY)
VMEM = pl.BlockSpec(memory_space=pltpu.VMEM)
HBM = pl.BlockSpec(memory_space=pltpu.HBM)


def swap(x, axis, bit):
    n = lax.axis_size(axis)
    return lax.ppermute(x, axis, [(i, i ^ bit) for i in range(n)])


def peer(k, e):
    return jnp.bitwise_xor(lax.axis_index("fsdp"), 2 * k + e)


def pick_kernel(groups, other, grads, *refs):
    outs, sem = refs[:-1], refs[-1]
    slabs = grads.shape[1]
    block = outs[0].shape[-1]
    per_rep = lax.axis_size("fsdp") // slabs
    rep = jnp.bitwise_xor(lax.axis_index("rep"), 1 if other else 0)
    copies = []
    for group, out in zip(groups, outs):
        for i, k in enumerate(group):
            for j in range(out.shape[1]):
                for e in range(2):
                    to = peer(k, e)
                    column = jnp.bitwise_xor(rep, 2 * j) * per_rep + to // slabs
                    start = pl.multiple_of(column * block, block)
                    copies.append(
                        pltpu.make_async_copy(
                            grads.at[0, lax.rem(to, slabs), :, pl.ds(start, block)],
                            out.at[i, j, e],
                            sem,
                        )
                    )
    for copy in copies:
        copy.start()
    for copy in copies:
        copy.wait()


def pick(grads, groups, other):
    rows = grads.shape[2]
    block = rows * lax.axis_size("fsdp")
    shapes = [
        jax.ShapeDtypeStruct((len(g), lax.axis_size("rep") // 2, 2, rows, block), grads.dtype)
        for g in groups
    ]
    return pl.pallas_call(
        functools.partial(pick_kernel, groups, other),
        out_shape=shapes,
        in_specs=[HBM],
        out_specs=[ANY] * len(groups),
        scratch_shapes=[pltpu.SemaphoreType.DMA],
        compiler_params=pltpu.CompilerParams(vmem_limit_bytes=4 * MIB),
        cost_estimate=pl.CostEstimate(flops=0, bytes_accessed=2 * MIB, transcendentals=0),
        name="pick_other" if other else "pick_own",
    )(pltpu.with_memory_space_constraint(grads, pltpu.HBM))


def place(k, e, rows):
    return pl.ds(pl.multiple_of(peer(k, e) * rows, rows), rows)


def main_kernel(spots, out_spots, *refs):
    ins, refs = refs[: len(spots)], refs[len(spots) :]
    left_root, right_root, accum = refs[:3]
    outs, refs = refs[3 : 3 + len(out_spots)], refs[3 + len(out_spots) :]
    block_out, lroot, rroot, acc, sems = refs
    rows = ins[0].shape[-2]

    lcopy = pltpu.make_async_copy(left_root.at[0], lroot, sems.at[1])
    rcopy = pltpu.make_async_copy(right_root.at[0], rroot, sems.at[2])
    acopy = pltpu.make_async_copy(accum.at[0], acc, sems.at[3])
    copies = [
        pltpu.make_async_copy(ref.at[i], block_out.at[place(k, e, rows)], sems.at[0])
        for ref, spot in zip(ins, spots)
        for i, (k, e) in enumerate(spot)
    ]
    lcopy.start()
    for copy in copies:
        copy.start()
    rcopy.start()
    acopy.start()
    lcopy.wait()
    for copy in copies:
        copy.wait()
    b = block_out[...]
    half = jnp.dot(lroot[...], b, preferred_element_type=jnp.float32).astype(jnp.bfloat16)
    rcopy.wait()
    precond = jnp.dot(half, rroot[...], preferred_element_type=jnp.float32)
    acopy.wait()
    wide = b.astype(jnp.float32)
    square = wide * wide
    ada_sq = jnp.sum(square / (acc[...] + square))
    pre_sq = jnp.sum(precond * precond)
    ratio = jnp.sqrt(ada_sq) / jnp.sqrt(pre_sq + 1e-06)
    lroot[...] = (ratio * precond).astype(jnp.bfloat16)
    for ref, spot in zip(outs, out_spots):
        for i, (k, e) in enumerate(spot):
            ref[i] = lroot[place(k, e, rows)]


def precondition(pieces, spots, out_spots, left_root, right_root, accum):
    side = left_root.shape[1]
    rows = pieces[0].shape[-2]
    outs = pl.pallas_call(
        functools.partial(main_kernel, spots, out_spots),
        out_shape=[
            jax.ShapeDtypeStruct((len(s), rows, side), jnp.bfloat16) for s in out_spots
        ]
        + [jax.ShapeDtypeStruct((side, side), jnp.bfloat16)],
        in_specs=[ANY] * (len(spots) + 3),
        out_specs=[VMEM] * (len(out_spots) + 1),
        scratch_shapes=[
            pltpu.VMEM((side, side), jnp.bfloat16),
            pltpu.VMEM((side, side), jnp.bfloat16),
            pltpu.VMEM((side, side), jnp.float32),
            pltpu.SemaphoreType.DMA((4,)),
        ],
        compiler_params=pltpu.CompilerParams(vmem_limit_bytes=16 * MIB),
        cost_estimate=pl.CostEstimate(
            flops=4 * side**3, bytes_accessed=12 * side * side, transcendentals=0
        ),
        name="precondition",
    )(*pieces, left_root, right_root, accum)
    return dict(zip(out_spots, outs)), outs[-1]


def stats_kernel(block, left, right, accum, left_out, right_out, accum_out):
    b = block[...]
    wide = b.astype(jnp.float32)
    accum_out[0] = accum[0] + wide * wide
    left_out[0] = left[0] + lax.dot_general(
        b, b, (((1,), (1,)), ((), ())), preferred_element_type=jnp.float32
    )
    right_out[0] = right[0] + lax.dot_general(
        b, b, (((0,), (0,)), ((), ())), preferred_element_type=jnp.float32
    )


def statistics(block, left, right, accum):
    shape = jax.ShapeDtypeStruct(left.shape, jnp.float32)
    side = left.shape[1]
    return pl.pallas_call(
        stats_kernel,
        out_shape=(shape,) * 3,
        in_specs=[VMEM] * 4,
        out_specs=(VMEM,) * 3,
        compiler_params=pltpu.CompilerParams(vmem_limit_bytes=20 * MIB),
        cost_estimate=pl.CostEstimate(
            flops=4 * side**3, bytes_accessed=26 * side * side, transcendentals=0
        ),
        name="statistics",
    )(block, left, right, accum)


def assemble_kernel(spots, *refs):
    ins, (update, sem) = refs[: len(spots)], refs[len(spots) :]
    slabs = update.shape[0]
    block = ins[0].shape[-1]
    copies = []
    for ref, spot in zip(ins, spots):
        for i, (k, e) in enumerate(spot):
            owner = peer(k, e)
            start = pl.multiple_of(owner // slabs * block, block)
            copies.append(
                pltpu.make_async_copy(
                    ref.at[i], update.at[lax.rem(owner, slabs), :, pl.ds(start, block)], sem
                )
            )
    for copy in copies:
        copy.start()
    for copy in copies:
        copy.wait()


def assemble(pieces, spots, shape):
    return pl.pallas_call(
        functools.partial(assemble_kernel, spots),
        out_shape=jax.ShapeDtypeStruct(shape, jnp.bfloat16),
        in_specs=[ANY] * len(pieces),
        out_specs=ANY,
        scratch_shapes=[pltpu.SemaphoreType.DMA],
        compiler_params=pltpu.CompilerParams(vmem_limit_bytes=4 * MIB),
        cost_estimate=pl.CostEstimate(flops=0, bytes_accessed=MIB, transcendentals=0),
        name="assemble",
    )(*pieces)


def far_pieces(peers):
    early = [k for k in range(peers - 1, 0, -1) if k % 2 == 0]
    late = [k for k in range(peers - 1, 0, -1) if k % 2 == 1]
    return early, late


def exchange(get, peers):
    early, late = far_pieces(peers)
    pieces, spots, crossing = [], [], {}
    for k in range(peers - 1, 0, -1):
        if k in early:
            near, far = get(k)
            come = swap(far, "fsdp", 1)
            both = swap(jnp.concatenate([near, come]), "fsdp", 2 * k)
            pieces.append(both)
            spots.append(((k, 0), (k, 1)))
        else:
            both = swap(get(k, whole=True), "fsdp", 2 * k)
            pieces.append(both)
            spots.append(((k, 0),))
            crossing[k] = both[1:]
    near, far = get(0)
    pieces.append(near)
    spots.append(((0, 0),))
    for group in ([0] + late[:-1], late[-1:]):
        lines = [far if k == 0 else crossing[k] for k in group]
        come = swap(jnp.concatenate(lines) if len(lines) > 1 else lines[0], "fsdp", 1)
        pieces.append(come)
        spots.append(tuple((k, 1) for k in group))
    return pieces, tuple(spots)


def total(terms):
    return sum(t.astype(jnp.float32) for t in terms).astype(jnp.bfloat16)


def body(grads, left_stat, right_stat, left_root, right_root, accum):
    rep_count, fsdp_count = lax.axis_size("rep"), lax.axis_size("fsdp")
    peers = fsdp_count // 2
    slabs, rows, width = grads.shape[1:]
    far = list(range(peers - 1, -1, -1))
    groups = (far[:1], far[1:2], far[2:])

    away = list(pick(grads, groups, True))
    for i, send in enumerate(away):
        if i > 0:
            send, away[i - 1] = lax.optimization_barrier((send, away[i - 1]))
        away[i] = swap(send, "rep", 1)
    mine = pick(grads, groups, False)

    summed = {}
    for group, theirs, ours in zip(groups, away, mine):
        for i, k in enumerate(group):
            terms, bit = [theirs[i], ours[i]], 1
            while 2 * bit < rep_count:
                bit *= 2
                pairs = [t.reshape((t.shape[0] // 2, 2) + t.shape[1:]) for t in terms]
                part = swap(total([p[:, 1] for p in pairs]), "rep", bit)
                terms = [p[:, 0] for p in pairs] + [part]
            summed[k] = [t[0] for t in terms]

    def summed_piece(k, whole=False):
        if whole:
            return total(summed[k])
        return [total([t[e : e + 1] for t in summed[k]]) for e in range(2)]

    pieces, spots = exchange(summed_piece, peers)

    early, late = far_pieces(peers)
    out_spots = tuple(((k, 0), (k, 1)) for k in late)
    out_spots += tuple(((k, e),) for k in early + [0] for e in range(2))
    scaled, block = precondition(pieces, spots, out_spots, left_root, right_root, accum)

    def scaled_piece(k, whole=False):
        return scaled[(k, 0), (k, 1)] if whole else [scaled[((k, e),)] for e in range(2)]

    pieces, spots = exchange(scaled_piece, peers)
    left_new, right_new, accum_new = statistics(block, left_stat, right_stat, accum)
    update = assemble(pieces, spots, (slabs, rows, width // rep_count))
    return (update, left_new, right_new, accum_new)


def solution(mesh):
    owned = P(("rep", "fsdp"), None, None)
    return jax.shard_map(
        body,
        mesh=mesh,
        in_specs=(P("rep", None, "fsdp", None),) + (owned,) * 5,
        out_specs=(P(None, "fsdp", "rep"),) + (owned,) * 3,
        check_vma=False,
    )
```

```python
import functools

import jax
import jax.numpy as jnp
from jax import lax
from jax.experimental import pallas as pl
from jax.experimental.pallas import tpu as pltpu
from jax.sharding import PartitionSpec as P

MIB = 1024 * 1024
ANY = pl.BlockSpec(memory_space=pl.ANY)
VMEM = pl.BlockSpec(memory_space=pltpu.VMEM)


def swap(x, axis, bit):
    n = lax.axis_size(axis)
    return lax.ppermute(x, axis, [(i, i ^ bit) for i in range(n)])


def peer(k, e):
    return jnp.bitwise_xor(lax.axis_index("fsdp"), 2 * k + e)


def pick_kernel(other, grads, out, sem):
    slabs = grads.shape[1]
    block = out.shape[-1]
    per_rep = lax.axis_size("fsdp") // slabs
    rep = jnp.bitwise_xor(lax.axis_index("rep"), 1 if other else 0)
    copies = []
    for k in range(out.shape[0]):
        for j in range(out.shape[1]):
            for e in range(2):
                to = peer(k, e)
                column = jnp.bitwise_xor(rep, 2 * j) * per_rep + to // slabs
                start = pl.multiple_of(column * block, block)
                copies.append(
                    pltpu.make_async_copy(
                        grads.at[0, lax.rem(to, slabs), :, pl.ds(start, block)],
                        out.at[k, j, e],
                        sem,
                    )
                )
    for copy in copies:
        copy.start()
    for copy in copies:
        copy.wait()


def pick(grads, other):
    rows = grads.shape[2]
    fsdp_count = lax.axis_size("fsdp")
    shape = (fsdp_count // 2, lax.axis_size("rep") // 2, 2, rows, rows * fsdp_count)
    return pl.pallas_call(
        functools.partial(pick_kernel, other),
        out_shape=jax.ShapeDtypeStruct(shape, grads.dtype),
        in_specs=[ANY],
        out_specs=ANY,
        scratch_shapes=[pltpu.SemaphoreType.DMA],
        compiler_params=pltpu.CompilerParams(vmem_limit_bytes=4 * MIB),
        cost_estimate=pl.CostEstimate(flops=0, bytes_accessed=2 * MIB, transcendentals=0),
        name="pick_other" if other else "pick_own",
    )(pltpu.with_memory_space_constraint(grads, pltpu.HBM))


def place(k, e, rows):
    return pl.ds(pl.multiple_of(peer(k, e) * rows, rows), rows)


def main_kernel(spots, *refs):
    ins, refs = refs[: len(spots)], refs[len(spots) :]
    left_root, right_root, accum = refs[:3]
    outs, refs = refs[3 : 3 + len(spots)], refs[3 + len(spots) :]
    block_out, lroot, rroot, acc, sems = refs
    rows = ins[0].shape[-2]

    lcopy = pltpu.make_async_copy(left_root.at[0], lroot, sems.at[1])
    rcopy = pltpu.make_async_copy(right_root.at[0], rroot, sems.at[2])
    acopy = pltpu.make_async_copy(accum.at[0], acc, sems.at[3])
    copies = [
        pltpu.make_async_copy(ref.at[i], block_out.at[place(k, e, rows)], sems.at[0])
        for ref, spot in zip(ins, spots)
        for i, (k, e) in enumerate(spot)
    ]
    lcopy.start()
    for copy in copies:
        copy.start()
    rcopy.start()
    acopy.start()
    lcopy.wait()
    for copy in copies:
        copy.wait()
    b = block_out[...]
    half = jnp.dot(lroot[...], b, preferred_element_type=jnp.float32).astype(jnp.bfloat16)
    rcopy.wait()
    precond = jnp.dot(half, rroot[...], preferred_element_type=jnp.float32)
    acopy.wait()
    wide = b.astype(jnp.float32)
    square = wide * wide
    ada_sq = jnp.sum(square / (acc[...] + square))
    pre_sq = jnp.sum(precond * precond)
    ratio = jnp.sqrt(ada_sq) / jnp.sqrt(pre_sq + 1e-06)
    lroot[...] = (ratio * precond).astype(jnp.bfloat16)
    for ref, spot in zip(outs, spots):
        for i, (k, e) in enumerate(spot):
            ref[i] = lroot[place(k, e, rows)]


def precondition(pieces, spots, left_root, right_root, accum):
    side = left_root.shape[1]
    rows = pieces[0].shape[-2]
    outs = pl.pallas_call(
        functools.partial(main_kernel, spots),
        out_shape=[
            jax.ShapeDtypeStruct((len(s), rows, side), jnp.bfloat16) for s in spots
        ]
        + [jax.ShapeDtypeStruct((side, side), jnp.bfloat16)],
        in_specs=[ANY] * (len(spots) + 3),
        out_specs=[VMEM] * (len(spots) + 1),
        scratch_shapes=[
            pltpu.VMEM((side, side), jnp.bfloat16),
            pltpu.VMEM((side, side), jnp.bfloat16),
            pltpu.VMEM((side, side), jnp.float32),
            pltpu.SemaphoreType.DMA((4,)),
        ],
        compiler_params=pltpu.CompilerParams(vmem_limit_bytes=16 * MIB),
        cost_estimate=pl.CostEstimate(
            flops=4 * side**3, bytes_accessed=12 * side * side, transcendentals=0
        ),
        name="precondition",
    )(*pieces, left_root, right_root, accum)
    return dict(zip(spots, outs)), outs[-1]


def stats_kernel(block, left, right, accum, left_out, right_out, accum_out):
    b = block[...]
    wide = b.astype(jnp.float32)
    accum_out[0] = accum[0] + wide * wide
    left_out[0] = left[0] + lax.dot_general(
        b, b, (((1,), (1,)), ((), ())), preferred_element_type=jnp.float32
    )
    right_out[0] = right[0] + lax.dot_general(
        b, b, (((0,), (0,)), ((), ())), preferred_element_type=jnp.float32
    )


def statistics(block, left, right, accum):
    shape = jax.ShapeDtypeStruct(left.shape, jnp.float32)
    side = left.shape[1]
    return pl.pallas_call(
        stats_kernel,
        out_shape=(shape,) * 3,
        in_specs=[VMEM] * 4,
        out_specs=(VMEM,) * 3,
        compiler_params=pltpu.CompilerParams(vmem_limit_bytes=20 * MIB),
        cost_estimate=pl.CostEstimate(
            flops=4 * side**3, bytes_accessed=26 * side * side, transcendentals=0
        ),
        name="statistics",
    )(block, left, right, accum)


def assemble_kernel(spots, *refs):
    ins, (update, sem) = refs[: len(spots)], refs[len(spots) :]
    slabs = update.shape[0]
    block = ins[0].shape[-1]
    copies = []
    for ref, spot in zip(ins, spots):
        for i, (k, e) in enumerate(spot):
            owner = peer(k, e)
            start = pl.multiple_of(owner // slabs * block, block)
            copies.append(
                pltpu.make_async_copy(
                    ref.at[i], update.at[lax.rem(owner, slabs), :, pl.ds(start, block)], sem
                )
            )
    for copy in copies:
        copy.start()
    for copy in copies:
        copy.wait()


def assemble(pieces, spots, shape):
    return pl.pallas_call(
        functools.partial(assemble_kernel, spots),
        out_shape=jax.ShapeDtypeStruct(shape, jnp.bfloat16),
        in_specs=[ANY] * len(pieces),
        out_specs=ANY,
        scratch_shapes=[pltpu.SemaphoreType.DMA],
        compiler_params=pltpu.CompilerParams(vmem_limit_bytes=4 * MIB),
        cost_estimate=pl.CostEstimate(flops=0, bytes_accessed=MIB, transcendentals=0),
        name="assemble",
    )(*pieces)


def exchange(get, peers, far_last):
    ks = range(peers) if far_last else range(peers - 1, -1, -1)
    spots = [(k, e) for k in ks for e in (1, 0)]
    pieces = [swap(get(k, e), "fsdp", 2 * k + e) if k + e else get(k, e) for k, e in spots]
    return pieces, tuple((spot,) for spot in spots)


def wide(terms):
    return sum(t.astype(jnp.float32) for t in terms)


def total(terms):
    return wide(terms).astype(jnp.bfloat16)


def body(grads, left_stat, right_stat, left_root, right_root, accum):
    rep_count, fsdp_count = lax.axis_size("rep"), lax.axis_size("fsdp")
    peers = fsdp_count // 2
    slabs, rows, width = grads.shape[1:]

    theirs = swap(pick(grads, True), "rep", 1)
    ours = pick(grads, False)
    summed = {}
    for k in range(peers):
        terms, bit = [theirs[k], ours[k]], 1
        while 2 * bit < rep_count:
            bit *= 2
            pairs = [t.reshape((t.shape[0] // 2, 2) + t.shape[1:]) for t in terms]
            part = swap(total([p[:, 1] for p in pairs]), "rep", bit)
            kept = lax.optimization_barrier(wide([p[:, 0] for p in pairs]))
            terms = [kept, part]
        summed[k] = [t[0] for t in terms]

    def summed_piece(k, e):
        return total([t[e : e + 1] for t in summed[k]])

    pieces, spots = exchange(summed_piece, peers, True)

    scaled, block = precondition(pieces, spots, left_root, right_root, accum)
    pieces, spots = exchange(lambda k, e: scaled[((k, e),)], peers, False)
    left_new, right_new, accum_new = statistics(block, left_stat, right_stat, accum)
    update = assemble(pieces, spots, (slabs, rows, width // rep_count))
    return (update, left_new, right_new, accum_new)


def solution(mesh):
    owned = P(("rep", "fsdp"), None, None)
    return jax.shard_map(
        body,
        mesh=mesh,
        in_specs=(P("rep", None, "fsdp", None),) + (owned,) * 5,
        out_specs=(P(None, "fsdp", "rep"),) + (owned,) * 3,
        check_vma=False,
    )
```

```python
import functools

import jax
import jax.numpy as jnp
from jax import lax
from jax.experimental import pallas as pl
from jax.experimental.pallas import tpu as pltpu
from jax.sharding import PartitionSpec as P

MIB = 1024 * 1024
ANY = pl.BlockSpec(memory_space=pl.ANY)
VMEM = pl.BlockSpec(memory_space=pltpu.VMEM)


def swap(x, axis, bit):
    n = lax.axis_size(axis)
    return lax.ppermute(x, axis, [(i, i ^ bit) for i in range(n)])


def peer(k, e):
    return jnp.bitwise_xor(lax.axis_index("fsdp"), 2 * k + e)


def pick_kernel(groups, grads, *refs):
    outs, sem = refs[:-1], refs[-1]
    slabs = grads.shape[1]
    block = outs[0].shape[-1]
    per_rep = lax.axis_size("fsdp") // slabs
    copies = []
    for n, out in enumerate(outs):
        rep = jnp.bitwise_xor(lax.axis_index("rep"), 1 if n < len(groups) else 0)
        for i, k in enumerate(groups[n % len(groups)]):
            for j in range(out.shape[1]):
                for e in range(2):
                    to = peer(k, e)
                    column = jnp.bitwise_xor(rep, 2 * j) * per_rep + to // slabs
                    start = pl.multiple_of(column * block, block)
                    copies.append(
                        pltpu.make_async_copy(
                            grads.at[0, lax.rem(to, slabs), :, pl.ds(start, block)],
                            out.at[i, j, e],
                            sem,
                        )
                    )
    for copy in copies:
        copy.start()
    for copy in copies:
        copy.wait()


def pick(grads, groups):
    rows = grads.shape[2]
    block = rows * lax.axis_size("fsdp")
    reps = lax.axis_size("rep") // 2
    shapes = [jax.ShapeDtypeStruct((len(g), reps, 2, rows, block), grads.dtype) for g in groups]
    outs = pl.pallas_call(
        functools.partial(pick_kernel, groups),
        out_shape=shapes * 2,
        in_specs=[ANY],
        out_specs=[ANY] * (2 * len(groups)),
        scratch_shapes=[pltpu.SemaphoreType.DMA],
        compiler_params=pltpu.CompilerParams(vmem_limit_bytes=4 * MIB),
        cost_estimate=pl.CostEstimate(flops=0, bytes_accessed=4 * MIB, transcendentals=0),
        name="pick",
    )(pltpu.with_memory_space_constraint(grads, pltpu.HBM))
    return outs[: len(groups)], outs[len(groups) :]


def place(k, e, rows):
    return pl.ds(pl.multiple_of(peer(k, e) * rows, rows), rows)


def main_kernel(spots, *refs):
    ins, refs = refs[: len(spots)], refs[len(spots) :]
    left_root, right_root, accum = refs[:3]
    outs, (block_out, scaled) = refs[3:-2], refs[-2:]
    rows = ins[0].shape[-2]

    for ref, spot in zip(ins, spots):
        for i, (k, e) in enumerate(spot):
            block_out[place(k, e, rows)] = ref[i]
    b = block_out[...]
    half = jnp.dot(left_root[0], b, preferred_element_type=jnp.float32).astype(jnp.bfloat16)
    precond = jnp.dot(half, right_root[0], preferred_element_type=jnp.float32)
    wide = b.astype(jnp.float32)
    square = wide * wide
    ada_sq = jnp.sum(square / (accum[0] + square))
    pre_sq = jnp.sum(precond * precond)
    ratio = jnp.sqrt(ada_sq) / jnp.sqrt(pre_sq + 1e-06)
    scaled[...] = (ratio * precond).astype(jnp.bfloat16)
    for ref, spot in zip(outs, spots):
        for i, (k, e) in enumerate(spot):
            ref[i] = scaled[place(k, e, rows)]


def precondition(pieces, spots, left_root, right_root, accum):
    side = left_root.shape[1]
    rows = pieces[0].shape[-2]
    outs = pl.pallas_call(
        functools.partial(main_kernel, spots),
        out_shape=[
            jax.ShapeDtypeStruct((len(s), rows, side), jnp.bfloat16) for s in spots
        ]
        + [jax.ShapeDtypeStruct((side, side), jnp.bfloat16)],
        in_specs=[VMEM] * (len(spots) + 3),
        out_specs=[VMEM] * (len(spots) + 1),
        scratch_shapes=[pltpu.VMEM((side, side), jnp.bfloat16)],
        compiler_params=pltpu.CompilerParams(vmem_limit_bytes=16 * MIB),
        cost_estimate=pl.CostEstimate(
            flops=4 * side**3, bytes_accessed=12 * side * side, transcendentals=0
        ),
        name="precondition",
    )(*pieces, left_root, right_root, accum)
    return dict(zip(spots, outs)), outs[-1]


def stats_kernel(block, left, right, accum, left_out, right_out, accum_out):
    b = block[...]
    wide = b.astype(jnp.float32)
    accum_out[0] = accum[0] + wide * wide
    left_out[0] = left[0] + lax.dot_general(
        b, b, (((1,), (1,)), ((), ())), preferred_element_type=jnp.float32
    )
    right_out[0] = right[0] + lax.dot_general(
        b, b, (((0,), (0,)), ((), ())), preferred_element_type=jnp.float32
    )


def statistics(block, left, right, accum):
    shape = jax.ShapeDtypeStruct(left.shape, jnp.float32)
    side = left.shape[1]
    return pl.pallas_call(
        stats_kernel,
        out_shape=(shape,) * 3,
        in_specs=[VMEM] * 4,
        out_specs=(VMEM,) * 3,
        compiler_params=pltpu.CompilerParams(vmem_limit_bytes=20 * MIB),
        cost_estimate=pl.CostEstimate(
            flops=4 * side**3, bytes_accessed=26 * side * side, transcendentals=0
        ),
        name="statistics",
    )(block, left, right, accum)


def assemble_kernel(spots, *refs):
    ins, (update, sem) = refs[: len(spots)], refs[len(spots) :]
    slabs = update.shape[0]
    block = ins[0].shape[-1]
    copies = []
    for ref, spot in zip(ins, spots):
        for i, (k, e) in enumerate(spot):
            owner = peer(k, e)
            start = pl.multiple_of(owner // slabs * block, block)
            copies.append(
                pltpu.make_async_copy(
                    ref.at[i], update.at[lax.rem(owner, slabs), :, pl.ds(start, block)], sem
                )
            )
    for copy in copies:
        copy.start()
    for copy in copies:
        copy.wait()


def assemble(pieces, spots, shape):
    return pl.pallas_call(
        functools.partial(assemble_kernel, spots),
        out_shape=jax.ShapeDtypeStruct(shape, jnp.bfloat16),
        in_specs=[ANY] * len(pieces),
        out_specs=ANY,
        scratch_shapes=[pltpu.SemaphoreType.DMA],
        compiler_params=pltpu.CompilerParams(vmem_limit_bytes=4 * MIB),
        cost_estimate=pl.CostEstimate(flops=0, bytes_accessed=MIB, transcendentals=0),
        name="assemble",
    )(*pieces)


def exchange(get, peers, far_last):
    ks = range(peers) if far_last else range(peers - 1, -1, -1)
    spots = [(k, e) for k in ks for e in (1, 0)]
    pieces = [swap(get(k, e), "fsdp", 2 * k + e) if k + e else get(k, e) for k, e in spots]
    return pieces, tuple((spot,) for spot in spots)


def wide(terms):
    return sum(t.astype(jnp.float32) for t in terms)


def total(terms):
    return wide(terms).astype(jnp.bfloat16)


def body(grads, left_stat, right_stat, left_root, right_root, accum):
    rep_count, fsdp_count = lax.axis_size("rep"), lax.axis_size("fsdp")
    peers = fsdp_count // 2
    slabs, rows, width = grads.shape[1:]

    groups = [[0, 1]] + [[k] for k in range(2, peers)]
    away, mine = pick(grads, groups)
    summed = {}
    for group, theirs, ours in zip(groups, away, mine):
        terms, bit = [swap(theirs, "rep", 1), ours], 1
        while 2 * bit < rep_count:
            bit *= 2
            pairs = [t.reshape((t.shape[0], t.shape[1] // 2, 2) + t.shape[2:]) for t in terms]
            part = swap(total([p[:, :, 1] for p in pairs]), "rep", bit)
            kept = lax.optimization_barrier(wide([p[:, :, 0] for p in pairs]))
            terms = [kept, part]
        for i, k in enumerate(group):
            summed[k] = [t[i, 0] for t in terms]

    def summed_piece(k, e):
        return total([t[e : e + 1] for t in summed[k]])

    pieces, spots = exchange(summed_piece, peers, True)

    scaled, block = precondition(pieces, spots, left_root, right_root, accum)
    pieces, spots = exchange(lambda k, e: scaled[((k, e),)], peers, False)
    left_new, right_new, accum_new = statistics(block, left_stat, right_stat, accum)
    update = assemble(pieces, spots, (slabs, rows, width // rep_count))
    return (update, left_new, right_new, accum_new)


def solution(mesh):
    owned = P(("rep", "fsdp"), None, None)
    return jax.shard_map(
        body,
        mesh=mesh,
        in_specs=(P("rep", None, "fsdp", None),) + (owned,) * 5,
        out_specs=(P(None, "fsdp", "rep"),) + (owned,) * 3,
        check_vma=False,
    )
```

```python
import functools

import jax
import jax.numpy as jnp
from jax import lax
from jax.experimental import pallas as pl
from jax.experimental.pallas import tpu as pltpu
from jax.sharding import PartitionSpec as P

MIB = 1024 * 1024
ANY = pl.BlockSpec(memory_space=pl.ANY)
VMEM = pl.BlockSpec(memory_space=pltpu.VMEM)


def swap(x, axis, bit):
    n = lax.axis_size(axis)
    return lax.ppermute(x, axis, [(i, i ^ bit) for i in range(n)])


def peer(k, e):
    return jnp.bitwise_xor(lax.axis_index("fsdp"), 2 * k + e)


def pick_kernel(groups, grads, *refs):
    outs, sem = refs[:-1], refs[-1]
    slabs = grads.shape[1]
    block = outs[0].shape[-1]
    per_rep = lax.axis_size("fsdp") // slabs
    copies = []
    for n, out in enumerate(outs):
        rep = jnp.bitwise_xor(lax.axis_index("rep"), 1 if n < len(groups) else 0)
        for i, k in enumerate(groups[n % len(groups)]):
            for j in range(out.shape[1]):
                for e in range(2):
                    to = peer(k, e)
                    column = jnp.bitwise_xor(rep, 2 * j) * per_rep + to // slabs
                    start = pl.multiple_of(column * block, block)
                    copies.append(
                        pltpu.make_async_copy(
                            grads.at[0, lax.rem(to, slabs), :, pl.ds(start, block)],
                            out.at[i, j, e],
                            sem,
                        )
                    )
    for copy in copies:
        copy.start()
    for copy in copies:
        copy.wait()


def pick(grads, groups):
    rows = grads.shape[2]
    block = rows * lax.axis_size("fsdp")
    reps = lax.axis_size("rep") // 2
    shapes = [jax.ShapeDtypeStruct((len(g), reps, 2, rows, block), grads.dtype) for g in groups]
    outs = pl.pallas_call(
        functools.partial(pick_kernel, groups),
        out_shape=shapes * 2,
        in_specs=[ANY],
        out_specs=[ANY] * (2 * len(groups)),
        scratch_shapes=[pltpu.SemaphoreType.DMA],
        compiler_params=pltpu.CompilerParams(vmem_limit_bytes=4 * MIB),
        cost_estimate=pl.CostEstimate(flops=0, bytes_accessed=4 * MIB, transcendentals=0),
        name="pick",
    )(pltpu.with_memory_space_constraint(grads, pltpu.HBM))
    return outs[: len(groups)], outs[len(groups) :]


def place(k, e, rows):
    return pl.ds(pl.multiple_of(peer(k, e) * rows, rows), rows)


def main_kernel(spots, *refs):
    ins, refs = refs[: len(spots)], refs[len(spots) :]
    left_root, right_root, accum = refs[:3]
    outs, (block_out, scaled) = refs[3:-2], refs[-2:]
    rows = ins[0].shape[-2]

    for ref, spot in zip(ins, spots):
        for i, (k, e) in enumerate(spot):
            block_out[place(k, e, rows)] = ref[i]
    b = block_out[...]
    half = jnp.dot(left_root[0], b, preferred_element_type=jnp.float32).astype(jnp.bfloat16)
    precond = jnp.dot(half, right_root[0], preferred_element_type=jnp.float32)
    wide = b.astype(jnp.float32)
    square = wide * wide
    ada_sq = jnp.sum(square / (accum[0] + square))
    pre_sq = jnp.sum(precond * precond)
    ratio = jnp.sqrt(ada_sq) / jnp.sqrt(pre_sq + 1e-06)
    scaled[...] = (ratio * precond).astype(jnp.bfloat16)
    for ref, spot in zip(outs, spots):
        for i, (k, e) in enumerate(spot):
            ref[i] = scaled[place(k, e, rows)]


def precondition(pieces, spots, left_root, right_root, accum):
    side = left_root.shape[1]
    rows = pieces[0].shape[-2]
    outs = pl.pallas_call(
        functools.partial(main_kernel, spots),
        out_shape=[
            jax.ShapeDtypeStruct((len(s), rows, side), jnp.bfloat16) for s in spots
        ]
        + [jax.ShapeDtypeStruct((side, side), jnp.bfloat16)],
        in_specs=[VMEM] * (len(spots) + 3),
        out_specs=[VMEM] * (len(spots) + 1),
        scratch_shapes=[pltpu.VMEM((side, side), jnp.bfloat16)],
        compiler_params=pltpu.CompilerParams(vmem_limit_bytes=16 * MIB),
        cost_estimate=pl.CostEstimate(
            flops=4 * side**3, bytes_accessed=12 * side * side, transcendentals=0
        ),
        name="precondition",
    )(*pieces, left_root, right_root, accum)
    return dict(zip(spots, outs)), outs[-1]


def stats_kernel(block, left, right, accum, left_out, right_out, accum_out):
    b = block[...]
    wide = b.astype(jnp.float32)
    accum_out[0] = accum[0] + wide * wide
    left_out[0] = left[0] + lax.dot_general(
        b, b, (((1,), (1,)), ((), ())), preferred_element_type=jnp.float32
    )
    right_out[0] = right[0] + lax.dot_general(
        b, b, (((0,), (0,)), ((), ())), preferred_element_type=jnp.float32
    )


def statistics(block, left, right, accum):
    shape = jax.ShapeDtypeStruct(left.shape, jnp.float32)
    side = left.shape[1]
    return pl.pallas_call(
        stats_kernel,
        out_shape=(shape,) * 3,
        in_specs=[VMEM] * 4,
        out_specs=(VMEM,) * 3,
        compiler_params=pltpu.CompilerParams(vmem_limit_bytes=20 * MIB),
        cost_estimate=pl.CostEstimate(
            flops=4 * side**3, bytes_accessed=26 * side * side, transcendentals=0
        ),
        name="statistics",
    )(block, left, right, accum)


def assemble_kernel(spots, *refs):
    ins, (update, sem) = refs[: len(spots)], refs[len(spots) :]
    slabs = update.shape[0]
    block = ins[0].shape[-1]
    copies = []
    for ref, spot in zip(ins, spots):
        for i, (k, e) in enumerate(spot):
            owner = peer(k, e)
            start = pl.multiple_of(owner // slabs * block, block)
            copies.append(
                pltpu.make_async_copy(
                    ref.at[i], update.at[lax.rem(owner, slabs), :, pl.ds(start, block)], sem
                )
            )
    for copy in copies:
        copy.start()
    for copy in copies:
        copy.wait()


def assemble(pieces, spots, shape):
    return pl.pallas_call(
        functools.partial(assemble_kernel, spots),
        out_shape=jax.ShapeDtypeStruct(shape, jnp.bfloat16),
        in_specs=[ANY] * len(pieces),
        out_specs=ANY,
        scratch_shapes=[pltpu.SemaphoreType.DMA],
        compiler_params=pltpu.CompilerParams(vmem_limit_bytes=4 * MIB),
        cost_estimate=pl.CostEstimate(flops=0, bytes_accessed=MIB, transcendentals=0),
        name="assemble",
    )(*pieces)


def exchange(get, peers, far_last):
    ks = [0, 1, *range(peers - 1, 1, -1)] if far_last else range(peers - 1, -1, -1)
    spots = [(k, e) for k in ks for e in ((0, 1) if far_last else (1, 0))]
    pieces = [swap(get(k, e), "fsdp", 2 * k + e) if k + e else get(k, e) for k, e in spots]
    return pieces, tuple((spot,) for spot in spots)


def wide(terms):
    return sum(t.astype(jnp.float32) for t in terms)


def total(terms):
    return wide(terms).astype(jnp.bfloat16)


def body(grads, left_stat, right_stat, left_root, right_root, accum):
    rep_count, fsdp_count = lax.axis_size("rep"), lax.axis_size("fsdp")
    peers = fsdp_count // 2
    slabs, rows, width = grads.shape[1:]

    groups = [[0, 1]] + [[k] for k in range(peers - 1, 1, -1)]
    away, mine = pick(grads, groups)
    summed = {}
    for group, theirs, ours in zip(groups, away, mine):
        theirs = swap(theirs, "rep", 1)
        for es in [[0], [1]] if group[-1] == 2 else [[0, 1]]:
            terms, bit = [a[:, :, es[0] : es[-1] + 1] for a in (theirs, ours)], 1
            while 2 * bit < rep_count:
                bit *= 2
                pairs = [t.reshape((t.shape[0], t.shape[1] // 2, 2) + t.shape[2:]) for t in terms]
                part = swap(total([p[:, :, 1] for p in pairs]), "rep", bit)
                kept = lax.optimization_barrier(wide([p[:, :, 0] for p in pairs]))
                terms = [kept, part]
            for i, k in enumerate(group):
                for j, e in enumerate(es):
                    summed[k, e] = [t[i, 0, j : j + 1] for t in terms]

    def summed_piece(k, e):
        return total(summed[k, e])

    pieces, spots = exchange(summed_piece, peers, True)

    scaled, block = precondition(pieces, spots, left_root, right_root, accum)
    pieces, spots = exchange(lambda k, e: scaled[((k, e),)], peers, False)
    left_new, right_new, accum_new = statistics(block, left_stat, right_stat, accum)
    update = assemble(pieces, spots, (slabs, rows, width // rep_count))
    return (update, left_new, right_new, accum_new)


def solution(mesh):
    owned = P(("rep", "fsdp"), None, None)
    return jax.shard_map(
        body,
        mesh=mesh,
        in_specs=(P("rep", None, "fsdp", None),) + (owned,) * 5,
        out_specs=(P(None, "fsdp", "rep"),) + (owned,) * 3,
        check_vma=False,
    )
```

```python
import functools

import jax
import jax.numpy as jnp
from jax import lax
from jax.experimental import pallas as pl
from jax.experimental.pallas import tpu as pltpu
from jax.sharding import PartitionSpec as P

MIB = 1024 * 1024
ANY = pl.BlockSpec(memory_space=pl.ANY)
VMEM = pl.BlockSpec(memory_space=pltpu.VMEM)


def swap(x, axis, bit):
    n = lax.axis_size(axis)
    return lax.ppermute(x, axis, [(i, i ^ bit) for i in range(n)])


def peer(k, e):
    return jnp.bitwise_xor(lax.axis_index("fsdp"), 2 * k + e)


def further(d):
    n = lax.axis_size("fsdp")
    return lax.rem(lax.axis_index("fsdp") + (d + n), n)


def pick_kernel(groups, grads, *refs):
    outs, sem = refs[:-1], refs[-1]
    slabs = grads.shape[1]
    block = outs[0].shape[-1]
    per_rep = lax.axis_size("fsdp") // slabs
    copies = []
    for n, out in enumerate(outs):
        rep = jnp.bitwise_xor(lax.axis_index("rep"), 1 if n < len(groups) else 0)
        for i, k in enumerate(groups[n % len(groups)]):
            for j in range(out.shape[1]):
                for e in range(2):
                    to = peer(k, e)
                    column = jnp.bitwise_xor(rep, 2 * j) * per_rep + to // slabs
                    start = pl.multiple_of(column * block, block)
                    copies.append(
                        pltpu.make_async_copy(
                            grads.at[0, lax.rem(to, slabs), :, pl.ds(start, block)],
                            out.at[i, j, e],
                            sem,
                        )
                    )
    for copy in copies:
        copy.start()
    for copy in copies:
        copy.wait()


def pick(grads, groups):
    rows = grads.shape[2]
    block = rows * lax.axis_size("fsdp")
    reps = lax.axis_size("rep") // 2
    shapes = [jax.ShapeDtypeStruct((len(g), reps, 2, rows, block), grads.dtype) for g in groups]
    outs = pl.pallas_call(
        functools.partial(pick_kernel, groups),
        out_shape=shapes * 2,
        in_specs=[ANY],
        out_specs=[ANY] * (2 * len(groups)),
        scratch_shapes=[pltpu.SemaphoreType.DMA],
        compiler_params=pltpu.CompilerParams(vmem_limit_bytes=4 * MIB),
        cost_estimate=pl.CostEstimate(flops=0, bytes_accessed=4 * MIB, transcendentals=0),
        name="pick",
    )(pltpu.with_memory_space_constraint(grads, pltpu.HBM))
    return outs[: len(groups)], outs[len(groups) :]


def rows_of(device, rows):
    return pl.ds(pl.multiple_of(device * rows, rows), rows)


def main_kernel(spots, *refs):
    ins, (left_root, right_root, accum) = refs[: len(spots)], refs[len(spots) : len(spots) + 3]
    outs, (block_out, scaled) = refs[len(spots) + 3 : -2], refs[-2:]
    rows = ins[0].shape[-2]

    for ref, (k, e) in zip(ins, spots):
        block_out[rows_of(peer(k, e), rows)] = ref[0]
    b = block_out[...]
    half = jnp.dot(left_root[0], b, preferred_element_type=jnp.float32).astype(jnp.bfloat16)
    precond = jnp.dot(half, right_root[0], preferred_element_type=jnp.float32)
    wide = b.astype(jnp.float32)
    square = wide * wide
    ada_sq = jnp.sum(square / (accum[0] + square))
    pre_sq = jnp.sum(precond * precond)
    ratio = jnp.sqrt(ada_sq) / jnp.sqrt(pre_sq + 1e-06)
    scaled[...] = (ratio * precond).astype(jnp.bfloat16)
    for d, ref in enumerate(outs):
        ref[0] = scaled[rows_of(further(d), rows)]


def precondition(pieces, spots, left_root, right_root, accum):
    side = left_root.shape[1]
    piece = jax.ShapeDtypeStruct(pieces[0].shape, jnp.bfloat16)
    outs = pl.pallas_call(
        functools.partial(main_kernel, spots),
        out_shape=[piece] * len(pieces) + [jax.ShapeDtypeStruct((side, side), jnp.bfloat16)],
        in_specs=[VMEM] * (len(pieces) + 3),
        out_specs=[VMEM] * (len(pieces) + 1),
        scratch_shapes=[pltpu.VMEM((side, side), jnp.bfloat16)],
        compiler_params=pltpu.CompilerParams(vmem_limit_bytes=16 * MIB),
        cost_estimate=pl.CostEstimate(
            flops=4 * side**3, bytes_accessed=12 * side * side, transcendentals=0
        ),
        name="precondition",
    )(*pieces, left_root, right_root, accum)
    return outs[:-1], outs[-1]


def stats_kernel(block, left, right, accum, left_out, right_out, accum_out):
    b = block[...]
    wide = b.astype(jnp.float32)
    accum_out[0] = accum[0] + wide * wide
    left_out[0] = left[0] + lax.dot_general(
        b, b, (((1,), (1,)), ((), ())), preferred_element_type=jnp.float32
    )
    right_out[0] = right[0] + lax.dot_general(
        b, b, (((0,), (0,)), ((), ())), preferred_element_type=jnp.float32
    )


def statistics(block, left, right, accum):
    shape = jax.ShapeDtypeStruct(left.shape, jnp.float32)
    side = left.shape[1]
    return pl.pallas_call(
        stats_kernel,
        out_shape=(shape,) * 3,
        in_specs=[VMEM] * 4,
        out_specs=(VMEM,) * 3,
        compiler_params=pltpu.CompilerParams(vmem_limit_bytes=20 * MIB),
        cost_estimate=pl.CostEstimate(
            flops=4 * side**3, bytes_accessed=26 * side * side, transcendentals=0
        ),
        name="statistics",
    )(block, left, right, accum)


def assemble_kernel(*refs):
    pieces, (update, sem) = refs[:-2], refs[-2:]
    slabs = update.shape[0]
    block = pieces[0].shape[-1]
    copies = []
    for d, ref in enumerate(pieces):
        owner = further(-d)
        start = pl.multiple_of(owner // slabs * block, block)
        copies.append(
            pltpu.make_async_copy(
                ref.at[0], update.at[lax.rem(owner, slabs), :, pl.ds(start, block)], sem
            )
        )
    for copy in copies:
        copy.start()
    for copy in copies:
        copy.wait()


def assemble(pieces, shape):
    return pl.pallas_call(
        assemble_kernel,
        out_shape=jax.ShapeDtypeStruct(shape, jnp.bfloat16),
        in_specs=[ANY] * len(pieces),
        out_specs=ANY,
        scratch_shapes=[pltpu.SemaphoreType.DMA],
        compiler_params=pltpu.CompilerParams(vmem_limit_bytes=4 * MIB),
        cost_estimate=pl.CostEstimate(flops=0, bytes_accessed=MIB, transcendentals=0),
        name="assemble",
    )(*pieces)


def wide(terms):
    return sum(t.astype(jnp.float32) for t in terms)


def total(terms):
    return wide(terms).astype(jnp.bfloat16)


def body(grads, left_stat, right_stat, left_root, right_root, accum):
    rep_count, fsdp_count = lax.axis_size("rep"), lax.axis_size("fsdp")
    peers = fsdp_count // 2
    slabs, rows, width = grads.shape[1:]

    groups = [[0, 1]] + [[k] for k in range(peers - 1, 1, -1)]
    away, mine = pick(grads, groups)
    summed = {}
    for group, theirs, ours in zip(groups, away, mine):
        theirs = swap(theirs, "rep", 1)
        for es in [[0], [1]] if group[-1] == 2 else [[0, 1]]:
            terms, bit = [a[:, :, es[0] : es[-1] + 1] for a in (theirs, ours)], 1
            while 2 * bit < rep_count:
                bit *= 2
                pairs = [t.reshape((t.shape[0], t.shape[1] // 2, 2) + t.shape[2:]) for t in terms]
                part = swap(total([p[:, :, 1] for p in pairs]), "rep", bit)
                kept = lax.optimization_barrier(wide([p[:, :, 0] for p in pairs]))
                terms = [kept, part]
            for i, k in enumerate(group):
                for j, e in enumerate(es):
                    summed[k, e] = [t[i, 0, j : j + 1] for t in terms]

    def summed_piece(k, e):
        return total(summed[k, e])

    spots = [(k, e) for k in (0, 1, *range(peers - 1, 1, -1)) for e in range(2)]
    pieces = [
        swap(summed_piece(k, e), "fsdp", 2 * k + e) if k + e else summed_piece(k, e)
        for k, e in spots
    ]
    scaled, block = precondition(pieces, spots, left_root, right_root, accum)
    returned = [
        lax.ppermute(a, "fsdp", [(i, (i + d) % fsdp_count) for i in range(fsdp_count)])
        for d, a in enumerate(scaled)
        if d > 0
    ]
    left_new, right_new, accum_new = statistics(block, left_stat, right_stat, accum)
    update = assemble([scaled[0], *returned], (slabs, rows, width // rep_count))
    return (update, left_new, right_new, accum_new)


def solution(mesh):
    owned = P(("rep", "fsdp"), None, None)
    return jax.shard_map(
        body,
        mesh=mesh,
        in_specs=(P("rep", None, "fsdp", None),) + (owned,) * 5,
        out_specs=(P(None, "fsdp", "rep"),) + (owned,) * 3,
        check_vma=False,
    )
```

```python
import functools

import jax
import jax.numpy as jnp
from jax import lax
from jax.experimental import pallas as pl
from jax.experimental.pallas import tpu as pltpu
from jax.sharding import PartitionSpec as P

MIB = 1024 * 1024
ANY = pl.BlockSpec(memory_space=pl.ANY)
VMEM = pl.BlockSpec(memory_space=pltpu.VMEM)


def swap(x, axis, bit):
    n = lax.axis_size(axis)
    return lax.ppermute(x, axis, [(i, i ^ bit) for i in range(n)])


def peer(k, e):
    return jnp.bitwise_xor(lax.axis_index("fsdp"), 2 * k + e)


def further(d):
    n = lax.axis_size("fsdp")
    return lax.rem(lax.axis_index("fsdp") + (d + n), n)


def pick_kernel(groups, grads, *refs):
    outs, sem = refs[:-1], refs[-1]
    slabs = grads.shape[1]
    block = outs[0].shape[-1]
    per_rep = lax.axis_size("fsdp") // slabs
    copies = []
    for n, out in enumerate(outs):
        rep = jnp.bitwise_xor(lax.axis_index("rep"), 1 if n < len(groups) else 0)
        for i, k in enumerate(groups[n % len(groups)]):
            for j in range(out.shape[1]):
                for e in range(2):
                    to = peer(k, e)
                    column = jnp.bitwise_xor(rep, 2 * j) * per_rep + to // slabs
                    start = pl.multiple_of(column * block, block)
                    copies.append(
                        pltpu.make_async_copy(
                            grads.at[0, lax.rem(to, slabs), :, pl.ds(start, block)],
                            out.at[i, j, e],
                            sem,
                        )
                    )
    for copy in copies:
        copy.start()
    for copy in copies:
        copy.wait()


def pick(grads, groups):
    rows = grads.shape[2]
    block = rows * lax.axis_size("fsdp")
    reps = lax.axis_size("rep") // 2
    shapes = [jax.ShapeDtypeStruct((len(g), reps, 2, rows, block), grads.dtype) for g in groups]
    outs = pl.pallas_call(
        functools.partial(pick_kernel, groups),
        out_shape=shapes * 2,
        in_specs=[ANY],
        out_specs=[ANY] * (2 * len(groups)),
        scratch_shapes=[pltpu.SemaphoreType.DMA],
        compiler_params=pltpu.CompilerParams(vmem_limit_bytes=4 * MIB),
        cost_estimate=pl.CostEstimate(flops=0, bytes_accessed=4 * MIB, transcendentals=0),
        name="pick",
    )(pltpu.with_memory_space_constraint(grads, pltpu.HBM))
    return outs[: len(groups)], outs[len(groups) :]


def rows_of(device, rows):
    return pl.ds(pl.multiple_of(device * rows, rows), rows)


def main_kernel(spots, *refs):
    ins, (left_root, right_root, accum) = refs[: len(spots)], refs[len(spots) : len(spots) + 3]
    outs, (block_out, scaled) = refs[len(spots) + 3 : -2], refs[-2:]
    rows = ins[0].shape[-2]

    for ref, (k, e) in zip(ins, spots):
        block_out[rows_of(peer(k, e), rows)] = ref[0]
    b = block_out[...]
    half = jnp.dot(left_root[0], b, preferred_element_type=jnp.float32).astype(jnp.bfloat16)
    precond = jnp.dot(half, right_root[0], preferred_element_type=jnp.float32)
    wide = b.astype(jnp.float32)
    square = wide * wide
    ada_sq = jnp.sum(square / (accum[0] + square))
    pre_sq = jnp.sum(precond * precond)
    ratio = jnp.sqrt(ada_sq) / jnp.sqrt(pre_sq + 1e-06)
    scaled[...] = (ratio * precond).astype(jnp.bfloat16)
    for d, ref in enumerate(outs):
        ref[0] = scaled[rows_of(further(d), rows)]


def precondition(pieces, spots, left_root, right_root, accum):
    side = left_root.shape[1]
    piece = jax.ShapeDtypeStruct(pieces[0].shape, jnp.bfloat16)
    outs = pl.pallas_call(
        functools.partial(main_kernel, spots),
        out_shape=[piece] * len(pieces) + [jax.ShapeDtypeStruct((side, side), jnp.bfloat16)],
        in_specs=[VMEM] * (len(pieces) + 3),
        out_specs=[VMEM] * (len(pieces) + 1),
        scratch_shapes=[pltpu.VMEM((side, side), jnp.bfloat16)],
        compiler_params=pltpu.CompilerParams(vmem_limit_bytes=16 * MIB),
        cost_estimate=pl.CostEstimate(
            flops=4 * side**3, bytes_accessed=12 * side * side, transcendentals=0
        ),
        name="precondition",
    )(*pieces, left_root, right_root, accum)
    return outs[:-1], outs[-1]


def stats_kernel(block, left, right, accum, *refs):
    outs, news, sems = refs[:3], refs[3:6], refs[6]
    copies = [pltpu.make_async_copy(news[i], outs[i].at[0], sems.at[i]) for i in range(3)]
    b = block[...]
    wide = b.astype(jnp.float32)
    news[2][...] = accum[0] + wide * wide
    copies[2].start()
    news[0][...] = left[0] + lax.dot_general(
        b, b, (((1,), (1,)), ((), ())), preferred_element_type=jnp.float32
    )
    copies[0].start()
    news[1][...] = right[0] + lax.dot_general(
        b, b, (((0,), (0,)), ((), ())), preferred_element_type=jnp.float32
    )
    copies[1].start()
    for copy in copies:
        copy.wait()


def statistics(block, left, right, accum):
    shape = jax.ShapeDtypeStruct(left.shape, jnp.float32)
    side = left.shape[1]
    return pl.pallas_call(
        stats_kernel,
        out_shape=(shape,) * 3,
        in_specs=[VMEM] * 4,
        out_specs=(ANY,) * 3,
        scratch_shapes=[pltpu.VMEM((side, side), jnp.float32)] * 3
        + [pltpu.SemaphoreType.DMA((3,))],
        compiler_params=pltpu.CompilerParams(vmem_limit_bytes=20 * MIB),
        cost_estimate=pl.CostEstimate(
            flops=4 * side**3, bytes_accessed=26 * side * side, transcendentals=0
        ),
        name="statistics",
    )(block, left, right, accum)


def assemble_kernel(*refs):
    pieces, (update, sem) = refs[:-2], refs[-2:]
    slabs = update.shape[0]
    block = pieces[0].shape[-1]
    copies = []
    for d, ref in enumerate(pieces):
        owner = further(-d)
        start = pl.multiple_of(owner // slabs * block, block)
        copies.append(
            pltpu.make_async_copy(
                ref.at[0], update.at[lax.rem(owner, slabs), :, pl.ds(start, block)], sem
            )
        )
    for copy in copies:
        copy.start()
    for copy in copies:
        copy.wait()


def assemble(pieces, shape):
    return pl.pallas_call(
        assemble_kernel,
        out_shape=jax.ShapeDtypeStruct(shape, jnp.bfloat16),
        in_specs=[ANY] * len(pieces),
        out_specs=ANY,
        scratch_shapes=[pltpu.SemaphoreType.DMA],
        compiler_params=pltpu.CompilerParams(vmem_limit_bytes=4 * MIB),
        cost_estimate=pl.CostEstimate(flops=0, bytes_accessed=MIB, transcendentals=0),
        name="assemble",
    )(*pieces)


def wide(terms):
    return sum(t.astype(jnp.float32) for t in terms)


def total(terms):
    return wide(terms).astype(jnp.bfloat16)


def body(grads, left_stat, right_stat, left_root, right_root, accum):
    rep_count, fsdp_count = lax.axis_size("rep"), lax.axis_size("fsdp")
    peers = fsdp_count // 2
    slabs, rows, width = grads.shape[1:]

    groups = [[0, 1]] + [[k] for k in range(peers - 1, 1, -1)]
    away, mine = pick(grads, groups)
    summed = {}
    for group, theirs, ours in zip(groups, away, mine):
        theirs = swap(theirs, "rep", 1)
        for es in [[0], [1]] if group[-1] == 2 else [[0, 1]]:
            terms, bit = [a[:, :, es[0] : es[-1] + 1] for a in (theirs, ours)], 1
            while 2 * bit < rep_count:
                bit *= 2
                pairs = [t.reshape((t.shape[0], t.shape[1] // 2, 2) + t.shape[2:]) for t in terms]
                part = swap(total([p[:, :, 1] for p in pairs]), "rep", bit)
                kept = lax.optimization_barrier(wide([p[:, :, 0] for p in pairs]))
                terms = [kept, part]
            for i, k in enumerate(group):
                for j, e in enumerate(es):
                    summed[k, e] = [t[i, 0, j : j + 1] for t in terms]

    def summed_piece(k, e):
        return total(summed[k, e])

    spots = [(k, e) for k in (0, 1, *range(peers - 1, 1, -1)) for e in range(2)]
    pieces = [
        swap(summed_piece(k, e), "fsdp", 2 * k + e) if k + e else summed_piece(k, e)
        for k, e in spots
    ]
    scaled, block = precondition(pieces, spots, left_root, right_root, accum)
    returned = [
        lax.ppermute(a, "fsdp", [(i, (i + d) % fsdp_count) for i in range(fsdp_count)])
        for d, a in enumerate(scaled)
        if d > 0
    ]
    left_new, right_new, accum_new = statistics(block, left_stat, right_stat, accum)
    update = assemble([scaled[0], *returned], (slabs, rows, width // rep_count))
    return (update, left_new, right_new, accum_new)


def solution(mesh):
    owned = P(("rep", "fsdp"), None, None)
    return jax.shard_map(
        body,
        mesh=mesh,
        in_specs=(P("rep", None, "fsdp", None),) + (owned,) * 5,
        out_specs=(P(None, "fsdp", "rep"),) + (owned,) * 3,
        check_vma=False,
    )
```

```python
import functools

import jax
import jax.numpy as jnp
from jax import lax
from jax.experimental import pallas as pl
from jax.experimental.pallas import tpu as pltpu
from jax.sharding import PartitionSpec as P

MIB = 1024 * 1024
ANY = pl.BlockSpec(memory_space=pl.ANY)
VMEM = pl.BlockSpec(memory_space=pltpu.VMEM)


def swap(x, axis, bit):
    n = lax.axis_size(axis)
    return lax.ppermute(x, axis, [(i, i ^ bit) for i in range(n)])


def peer(k, e):
    return jnp.bitwise_xor(lax.axis_index("fsdp"), 2 * k + e)


def further(d):
    n = lax.axis_size("fsdp")
    return lax.rem(lax.axis_index("fsdp") + (d + n), n)


def pick_kernel(groups, grads, *refs):
    outs, sem = refs[:-1], refs[-1]
    slabs = grads.shape[1]
    block = outs[0].shape[-1]
    per_rep = lax.axis_size("fsdp") // slabs
    copies = []
    for n, out in enumerate(outs):
        rep = jnp.bitwise_xor(lax.axis_index("rep"), 1 if n < len(groups) else 0)
        for i, k in enumerate(groups[n % len(groups)]):
            for j in range(out.shape[1]):
                for e in range(2):
                    to = peer(k, e)
                    column = jnp.bitwise_xor(rep, 2 * j) * per_rep + to // slabs
                    start = pl.multiple_of(column * block, block)
                    copies.append(
                        pltpu.make_async_copy(
                            grads.at[0, lax.rem(to, slabs), :, pl.ds(start, block)],
                            out.at[i, j, e],
                            sem,
                        )
                    )
    for copy in copies:
        copy.start()
    for copy in copies:
        copy.wait()


def pick(grads, groups):
    rows = grads.shape[2]
    block = rows * lax.axis_size("fsdp")
    reps = lax.axis_size("rep") // 2
    shapes = [jax.ShapeDtypeStruct((len(g), reps, 2, rows, block), grads.dtype) for g in groups]
    outs = pl.pallas_call(
        functools.partial(pick_kernel, groups),
        out_shape=shapes * 2,
        in_specs=[ANY],
        out_specs=[ANY] * (2 * len(groups)),
        scratch_shapes=[pltpu.SemaphoreType.DMA],
        compiler_params=pltpu.CompilerParams(vmem_limit_bytes=4 * MIB),
        cost_estimate=pl.CostEstimate(flops=0, bytes_accessed=4 * MIB, transcendentals=0),
        name="pick",
    )(pltpu.with_memory_space_constraint(grads, pltpu.HBM))
    return outs[: len(groups)], outs[len(groups) :]


def rows_of(device, rows):
    return pl.ds(pl.multiple_of(device * rows, rows), rows)


def main_kernel(spots, *refs):
    ins, (left_root, right_root, accum) = refs[: len(spots)], refs[len(spots) : len(spots) + 3]
    outs, block_out = refs[len(spots) + 3 : -1], refs[-1]
    rows = ins[0].shape[-2]

    for ref, (k, e) in zip(ins, spots):
        block_out[rows_of(peer(k, e), rows)] = ref[0]
    b = block_out[...]
    root = jnp.concatenate([left_root[0, rows_of(further(d), rows)] for d in range(len(outs))])
    half = jnp.dot(root, b, preferred_element_type=jnp.float32).astype(jnp.bfloat16)
    precond = jnp.dot(half, right_root[0], preferred_element_type=jnp.float32)
    wide = b.astype(jnp.float32)
    square = wide * wide
    ada_sq = jnp.sum(square / (accum[0] + square))
    pre_sq = jnp.sum(precond * precond)
    ratio = jnp.sqrt(ada_sq) / jnp.sqrt(pre_sq + 1e-06)
    for d, ref in enumerate(outs):
        ref[0] = (ratio * precond[d * rows : (d + 1) * rows]).astype(jnp.bfloat16)


def precondition(pieces, spots, left_root, right_root, accum):
    side = left_root.shape[1]
    piece = jax.ShapeDtypeStruct(pieces[0].shape, jnp.bfloat16)
    outs = pl.pallas_call(
        functools.partial(main_kernel, spots),
        out_shape=[piece] * len(pieces) + [jax.ShapeDtypeStruct((side, side), jnp.bfloat16)],
        in_specs=[VMEM] * (len(pieces) + 3),
        out_specs=[VMEM] * (len(pieces) + 1),
        compiler_params=pltpu.CompilerParams(vmem_limit_bytes=16 * MIB),
        cost_estimate=pl.CostEstimate(
            flops=4 * side**3, bytes_accessed=12 * side * side, transcendentals=0
        ),
        name="precondition",
    )(*pieces, left_root, right_root, accum)
    return outs[:-1], outs[-1]


def stats_kernel(block, left, right, accum, *refs):
    outs, news, sems = refs[:3], refs[3:6], refs[6]
    copies = [pltpu.make_async_copy(news[i], outs[i].at[0], sems.at[i]) for i in range(3)]
    b = block[...]
    wide = b.astype(jnp.float32)
    news[2][...] = accum[0] + wide * wide
    copies[2].start()
    news[0][...] = left[0] + lax.dot_general(
        b, b, (((1,), (1,)), ((), ())), preferred_element_type=jnp.float32
    )
    copies[0].start()
    news[1][...] = right[0] + lax.dot_general(
        b, b, (((0,), (0,)), ((), ())), preferred_element_type=jnp.float32
    )
    copies[1].start()
    for copy in copies:
        copy.wait()


def statistics(block, left, right, accum):
    shape = jax.ShapeDtypeStruct(left.shape, jnp.float32)
    side = left.shape[1]
    return pl.pallas_call(
        stats_kernel,
        out_shape=(shape,) * 3,
        in_specs=[VMEM] * 4,
        out_specs=(ANY,) * 3,
        scratch_shapes=[pltpu.VMEM((side, side), jnp.float32)] * 3
        + [pltpu.SemaphoreType.DMA((3,))],
        compiler_params=pltpu.CompilerParams(vmem_limit_bytes=20 * MIB),
        cost_estimate=pl.CostEstimate(
            flops=4 * side**3, bytes_accessed=26 * side * side, transcendentals=0
        ),
        name="statistics",
    )(block, left, right, accum)


def assemble_kernel(*refs):
    pieces, (update, sem) = refs[:-2], refs[-2:]
    slabs = update.shape[0]
    block = pieces[0].shape[-1]
    copies = []
    for d, ref in enumerate(pieces):
        owner = further(-d)
        start = pl.multiple_of(owner // slabs * block, block)
        copies.append(
            pltpu.make_async_copy(
                ref.at[0], update.at[lax.rem(owner, slabs), :, pl.ds(start, block)], sem
            )
        )
    for copy in copies:
        copy.start()
    for copy in copies:
        copy.wait()


def assemble(pieces, shape):
    return pl.pallas_call(
        assemble_kernel,
        out_shape=jax.ShapeDtypeStruct(shape, jnp.bfloat16),
        in_specs=[ANY] * len(pieces),
        out_specs=ANY,
        scratch_shapes=[pltpu.SemaphoreType.DMA],
        compiler_params=pltpu.CompilerParams(vmem_limit_bytes=4 * MIB),
        cost_estimate=pl.CostEstimate(flops=0, bytes_accessed=MIB, transcendentals=0),
        name="assemble",
    )(*pieces)


def wide(terms):
    return sum(t.astype(jnp.float32) for t in terms)


def total(terms):
    return wide(terms).astype(jnp.bfloat16)


def body(grads, left_stat, right_stat, left_root, right_root, accum):
    rep_count, fsdp_count = lax.axis_size("rep"), lax.axis_size("fsdp")
    peers = fsdp_count // 2
    slabs, rows, width = grads.shape[1:]

    groups = [[0, 1]] + [[k] for k in range(peers - 1, 1, -1)]
    away, mine = pick(grads, groups)
    summed = {}
    for group, theirs, ours in zip(groups, away, mine):
        theirs = swap(theirs, "rep", 1)
        for es in [[0], [1]] if group[-1] == 2 else [[0, 1]]:
            terms, bit = [a[:, :, es[0] : es[-1] + 1] for a in (theirs, ours)], 1
            while 2 * bit < rep_count:
                bit *= 2
                pairs = [t.reshape((t.shape[0], t.shape[1] // 2, 2) + t.shape[2:]) for t in terms]
                part = swap(total([p[:, :, 1] for p in pairs]), "rep", bit)
                kept = lax.optimization_barrier(wide([p[:, :, 0] for p in pairs]))
                terms = [kept, part]
            for i, k in enumerate(group):
                for j, e in enumerate(es):
                    summed[k, e] = [t[i, 0, j : j + 1] for t in terms]

    def summed_piece(k, e):
        return total(summed[k, e])

    spots = [(k, e) for k in (0, 1, *range(peers - 1, 1, -1)) for e in range(2)]
    pieces = [
        swap(summed_piece(k, e), "fsdp", 2 * k + e) if k + e else summed_piece(k, e)
        for k, e in spots
    ]
    scaled, block = precondition(pieces, spots, left_root, right_root, accum)
    returned = [
        lax.ppermute(a, "fsdp", [(i, (i + d) % fsdp_count) for i in range(fsdp_count)])
        for d, a in enumerate(scaled)
        if d > 0
    ]
    left_new, right_new, accum_new = statistics(block, left_stat, right_stat, accum)
    update = assemble([scaled[0], *returned], (slabs, rows, width // rep_count))
    return (update, left_new, right_new, accum_new)


def solution(mesh):
    owned = P(("rep", "fsdp"), None, None)
    return jax.shard_map(
        body,
        mesh=mesh,
        in_specs=(P("rep", None, "fsdp", None),) + (owned,) * 5,
        out_specs=(P(None, "fsdp", "rep"),) + (owned,) * 3,
        check_vma=False,
    )
```
